256 devices in a mesh: sensor: 32 (over y, x, z_lo), basis: 8 (over z_hi, core).
Axes of the slice: x: 4, y: 4, z: 8 (z_hi: 4, z_lo: 2; z = z_hi * 2 + z_lo), core: 2. Of those that a mesh axis runs over, the one named last changes fastest.
Arguments:
- readings: bfloat16 [98304, 128], P('sensor'), may hold values from -120 to 120
- design_tiles: bfloat16 [96, 8, 2, 1024, 512], P('sensor', 'basis'), may hold values from -0.0625 to 0.0625
- pattern: int32 [96, 8, 2], P('sensor', 'basis'), may hold values from 0 to 7, as said below
Outputs:
- solution: float32 [32768, 128], P('basis')
- search: float32 [32768, 128], P('basis')
- phi_bar: float32 [128], replicated
The draws below stay inside these ranges and needn't reach their ends.
Inputs may be any that keep to these rules, and one draw needn't show every extreme that they name: `pattern`: within one segment and one basis group the 2 entries are different.
All inputs are finite; a program needn't handle non-finite values.
Results may differ from the reference program's by a relative error of at most 0.02.
Values may be sent and summed in bfloat16 or wider, within the bound.
No kernel may reach another device: no remote copies, remote signals or barrier semaphores. Data moves between devices by JAX's collectives and lax.ppermute only.
A program may use at most 64 MiB of HBM per device.

```python
import math
import jax
import jax.numpy as jnp
from jax import lax

SEG = 1024
BW = 512
K = 128
CB_DEV = 8
NPB = 2
ITERS = 3
RBLOCKS = 96
ROWS = 98304
COLS = 32768
N_BASIS = 8


def draw_readings(key, part):
    key = jax.random.fold_in(key, 11)
    first, second, third = jax.random.split(key, 3)
    position = jnp.arange(ROWS, dtype=jnp.float32)[:, None]
    rising = 1.0 + 2.0 * position / ROWS
    row_scale = jnp.exp(jax.random.uniform(second, (ROWS, 1), jnp.float32) * math.log(10.0))
    col_scale = jnp.exp(jax.random.uniform(third, (1, K), jnp.float32) * math.log(10.0))
    noise = jax.random.normal(first, (ROWS, K), jnp.float32)
    noise = jnp.clip(noise, -4.0, 4.0)
    return (noise * row_scale * col_scale * rising * 0.1).astype(jnp.bfloat16)


def draw_pattern(key, part):
    key = jax.random.fold_in(key, 23)
    scores = jax.random.randint(key, (RBLOCKS, N_BASIS, CB_DEV), 0, 1 << 20, jnp.int32)
    column_ids = jnp.arange(CB_DEV, dtype=jnp.int32)[None, None, :]
    row_ids = jnp.arange(RBLOCKS, dtype=jnp.int32)[:, None, None]
    scores = scores * CB_DEV + column_ids
    scores = jnp.where((row_ids == 0) & (column_ids == CB_DEV - 1), -1, scores)
    scores = jnp.where((row_ids == 0) & (column_ids == 0), -2, scores)
    ranking = jnp.argsort(scores, axis=-1, stable=True)
    return ranking[:, :, :NPB].astype(jnp.int32)


def block_scale(key, dims, pieces, least, largest):
    factor_of = 1.0
    for dim, parts in pieces:
        heights = jax.random.uniform(jax.random.fold_in(jax.random.fold_in(key, 6), dim), (parts,), jnp.float32, least / len(pieces), largest / len(pieces))
        factor_of = factor_of * jnp.repeat(jnp.exp(heights), dims[dim] // parts).reshape((-1,) + (1,) * (len(dims) - 1 - dim))
    return factor_of


def normal_values(stream_key, dims, scale, limit, shards=(), kind=jnp.bfloat16):
    entries = jax.random.normal(stream_key, dims, jnp.float32) * scale
    if len(shards) > 0:
        entries = block_scale(stream_key, dims, shards, -0.22, 0.18) * entries
    return jnp.clip(entries, min=-limit, max=limit).astype(kind)


def setup_inputs(seed: int = 0) -> dict:
    splits = jax.random.split(jax.random.key(seed), 4)
    return {
        "readings": draw_readings(jax.random.fold_in(splits[3], 71), 0),
        "design_tiles": normal_values(splits[1], (RBLOCKS, N_BASIS, NPB, SEG, BW), (NPB * N_BASIS * BW) ** -0.5, 0.0625, ((0, 32), (1, 8))),
        "pattern": draw_pattern(jax.random.fold_in(splits[3], 71), 0),
    }


epsilon = 1e-06

def times_design(design_tiles, pattern, right_vec):
    right_bf = right_vec.astype(jnp.bfloat16).reshape(N_BASIS, CB_DEV, BW, K)
    groups = jnp.arange(N_BASIS, dtype=jnp.int32)[:, None]

    def row_block(pair):
        tile_row, slot_row = pair
        picked = right_bf[groups, slot_row]
        return jnp.einsum('gjsb,gjbk->sk', tile_row.astype(jnp.float32), picked.astype(jnp.float32))
    images = lax.map(row_block, (design_tiles, pattern))
    return images.reshape(ROWS, K)

def times_transpose(design_tiles, pattern, left_vec):
    left_bf = left_vec.astype(jnp.bfloat16).reshape(RBLOCKS, SEG, K)
    groups = jnp.arange(N_BASIS, dtype=jnp.int32)[:, None]

    def add_block(totals, triple):
        tile_row, slot_row, left_row = triple
        contrib = jnp.einsum('gjsb,sk->gjbk', tile_row.astype(jnp.float32), left_row.astype(jnp.float32))
        return (totals.at[groups, slot_row].add(contrib), None)
    totals = jnp.zeros((N_BASIS, CB_DEV, BW, K), jnp.float32)
    totals, unused = lax.scan(add_block, totals, (design_tiles, pattern, left_bf))
    return totals.reshape(COLS, K)

def column_norm(vectors):
    return jnp.sqrt(lax.optimization_barrier(jnp.sum(vectors * vectors, axis=0)) + epsilon)

def reference(readings, design_tiles, pattern):
    start = readings.astype(jnp.float32)
    beta_col = column_norm(start)
    left_vec = start / beta_col
    right_vec = times_transpose(design_tiles, pattern, left_vec)
    alpha_col = column_norm(right_vec)
    right_vec = right_vec / alpha_col
    search = right_vec
    solution = jnp.zeros_like(right_vec)
    phi_bar = beta_col
    rho_bar = alpha_col
    for sweep in range(ITERS):
        left_vec = times_design(design_tiles, pattern, right_vec) - alpha_col * left_vec
        beta_col = column_norm(left_vec)
        left_vec = left_vec / beta_col
        right_vec = times_transpose(design_tiles, pattern, left_vec) - beta_col * right_vec
        alpha_col = column_norm(right_vec)
        right_vec = right_vec / alpha_col
        rho_col = jnp.sqrt(rho_bar * rho_bar + beta_col * beta_col)
        cosine = rho_bar / rho_col
        sine = beta_col / rho_col
        theta_col = sine * alpha_col
        rho_bar = -cosine * alpha_col
        phi_col = cosine * phi_bar
        phi_bar = sine * phi_bar
        solution = solution + phi_col / rho_col * search
        search = right_vec - theta_col / rho_col * search
    return (solution, search, phi_bar)
```

```python
import functools

import jax
import jax.numpy as jnp
from jax import lax
from jax.experimental import pallas as pl
from jax.experimental.pallas import tpu as pltpu
from jax.sharding import PartitionSpec as P

CB_DEV = 8
ITERS = 3
EPS = 1e-06
LANES = 128
EXTRA = 16
VMEM_LIMIT = 24 * 1024 * 1024

BF = jnp.bfloat16
F32 = jnp.float32
Z_GROUPS = [[0, 2, 4, 6], [1, 3, 5, 7]]
CORE_PERM = [(i, i ^ 1) for i in range(8)]

VM = pl.BlockSpec(memory_space=pltpu.VMEM)
SM = pl.BlockSpec(memory_space=pltpu.SMEM)
ANY = pl.BlockSpec(memory_space=pl.ANY)


def sds(shape, dtype):
    return jax.ShapeDtypeStruct(shape, dtype)


def call(body, ins, outs, scratch=()):
    return pl.pallas_call(
        body,
        in_specs=ins,
        out_specs=[VM] * len(outs),
        out_shape=outs,
        scratch_shapes=scratch,
        compiler_params=pltpu.CompilerParams(vmem_limit_bytes=VMEM_LIMIT),
    )


def pack_row(row):
    high = row.astype(BF).astype(F32)
    low = row - high
    which = lax.broadcasted_iota(jnp.int32, (EXTRA, LANES), 0)
    tile = jnp.where(which == 0, high, jnp.where(which == 1, low, 0.0))
    return tile.astype(BF)


def unpack_rows(tile):
    wide = tile.astype(F32)
    if wide.ndim == 3:
        wide = jnp.sum(wide, axis=0)
    return jnp.sum(wide, axis=0, keepdims=True)


def across(row):
    return jnp.transpose(jnp.broadcast_to(row, (LANES, LANES)))


def tile_copies(tiles_ref, buf, sems, first):
    copies = []
    segs = []
    for i in range(6):
        q = lax.rem(first + i, 6)
        seg = lax.div(q, 2)
        top = pl.multiple_of(lax.rem(q, 2) * 512, 512)
        copies.append(
            pltpu.make_async_copy(tiles_ref.at[seg, :, pl.ds(top, 512), :], buf.at[i], sems.at[i])
        )
        segs.append(seg)
    return copies, segs


def forward_body(core_ref, slot_ref, g_ref, tiles_ref, send_ref, keep_ref, asq_ref, buf, sems):
    core = core_ref[0]
    copies, segs = tile_copies(tiles_ref, buf, sems, 3 * (1 - core))
    for c in copies:
        c.start()
    total = jnp.zeros((LANES, LANES), F32)
    for q in range(32):
        piece = g_ref[q].astype(F32)
        total = total + piece * piece
    asq = jnp.sum(jnp.transpose(total), axis=0, keepdims=True)
    asq_ref[...] = asq
    send_ref[1536:1552, :] = pack_row(asq)
    for i in range(6):
        copies[i].wait()
        acc = None
        for j in range(2):
            base = slot_ref[2 * segs[i] + j] * 4
            operand = jnp.concatenate([g_ref[base + t] for t in range(4)], axis=1)
            part = lax.dot_general(
                buf[i, j], operand, (((1,), (1,)), ((), ())), preferred_element_type=F32
            )
            acc = part if acc is None else acc + part
        if i < 3:
            send_ref[i * 512 : (i + 1) * 512, :] = acc.astype(BF)
        else:
            keep_ref[(i - 3) * 512 : (i - 2) * 512, :] = acc


def merge_body(keep_ref, recv_ref, asq_ref, msg_ref):
    tail = pack_row(asq_ref[...] + unpack_rows(recv_ref[1536:1552, :]))
    for z in range(4):
        part = keep_ref[z * 384 : (z + 1) * 384, :] + recv_ref[z * 384 : (z + 1) * 384, :].astype(F32)
        msg_ref[z, 0:384, :] = part.astype(BF)
        msg_ref[z, 384:400, :] = tail


def left_body(recv_ref, left_ref, bsq_ref, new_ref, msg_ref, asq_ref):
    asq = unpack_rows(recv_ref[:, 384:400, :])
    alpha = jnp.sqrt(asq + EPS)
    beta = jnp.sqrt(bsq_ref[...] + EPS)
    total = recv_ref[0, 0:384, :].astype(F32)
    for z in range(1, 4):
        total = total + recv_ref[z, 0:384, :].astype(F32)
    fresh = total * (1.0 / alpha) - (alpha / beta) * left_ref[...].astype(F32)
    new_ref[...] = fresh
    narrow = fresh.astype(BF)
    for z in range(4):
        msg_ref[z] = narrow
    asq_ref[...] = asq


def backward_body(core_ref, slot_ref, own_ref, other_ref, tiles_ref, msg_ref, buf, acc, sems):
    core = core_ref[0]
    copies, segs = tile_copies(tiles_ref, buf, sems, 3 * core)
    for c in copies:
        c.start()
    acc[...] = jnp.zeros_like(acc)
    bsq = jnp.zeros((1, LANES), F32)
    for ref in (own_ref, other_ref):
        for i in range(3):
            wide = ref[i * 512 : (i + 1) * 512, :].astype(F32)
            bsq = bsq + jnp.sum(wide * wide, axis=0, keepdims=True)
    for i in range(6):
        ref = own_ref if i < 3 else other_ref
        rows = (i % 3) * 512
        chunk = ref[rows : rows + 512, :]
        copies[i].wait()
        for j in range(2):
            slot = slot_ref[2 * segs[i] + j]
            part = lax.dot_general(
                chunk, buf[i, j], (((0,), (0,)), ((), ())), preferred_element_type=F32
            )
            acc[slot] += part
    tail = pack_row(bsq)
    for q in range(32):
        lane = (q % 4) * LANES
        msg_ref[q, 0:128, :] = acc[q // 4, :, lane : lane + LANES].astype(BF)
        msg_ref[q, 128:144, :] = tail


def share_body(first, recv_ref, *refs):
    if first:
        r_ref, msg_ref, bsq_ref = refs
    else:
        prev_ref, asq_ref, r_ref, msg_ref, bsq_ref = refs
    bsq = unpack_rows(recv_ref[:, 128:144, :])
    beta = jnp.sqrt(bsq + EPS)
    total = recv_ref[0, 0:128, :].astype(F32)
    for q in range(1, 32):
        total = total + recv_ref[q, 0:128, :].astype(F32)
    fresh = total * across(1.0 / beta)
    if not first:
        alpha = jnp.sqrt(asq_ref[...] + EPS)
        fresh = fresh - across(beta / alpha) * prev_ref[...]
    r_ref[...] = fresh
    narrow = fresh.astype(BF)
    for q in range(32):
        msg_ref[q] = narrow
    bsq_ref[...] = bsq


def square_body(g_ref, asq_ref):
    total = jnp.zeros((LANES, LANES), F32)
    for q in range(32):
        piece = g_ref[q].astype(F32)
        total = total + piece * piece
    asq_ref[...] = jnp.sum(jnp.transpose(total), axis=0, keepdims=True)


def final_body(coef_ref, g0_ref, g1_ref, g2_ref, g3_ref, sol_ref, search_ref):
    rows = coef_ref[...]
    wide = [across(rows[i : i + 1, :]) for i in range(7)]
    for q in range(32):
        g0 = g0_ref[q].astype(F32)
        g1 = g1_ref[q].astype(F32)
        g2 = g2_ref[q].astype(F32)
        g3 = g3_ref[q].astype(F32)
        sol = wide[0] * g0 + wide[1] * g1 + wide[2] * g2
        search = wide[3] * g0 + wide[4] * g1 + wide[5] * g2 + wide[6] * g3
        sol_ref[q * 128 : (q + 1) * 128, :] = jnp.transpose(sol)
        search_ref[q * 128 : (q + 1) * 128, :] = jnp.transpose(search)


def per_device(readings, design_tiles, pattern):
    tiles = design_tiles.reshape(3, 2, 1024, 512)
    slots = pattern.reshape(6)
    basis = lax.axis_index("basis")
    core = lax.rem(basis, 2).reshape(1).astype(jnp.int32)
    zero = jnp.zeros((1,), jnp.int32)
    z_hi = lax.div(basis, 2)
    sems = pltpu.SemaphoreType.DMA((6,))
    chunk_buf = pltpu.VMEM((6, 2, 512, 512), BF)

    forward = call(
        forward_body,
        [SM, SM, VM, ANY],
        [sds((1552, LANES), BF), sds((1536, LANES), F32), sds((1, LANES), F32)],
        [chunk_buf, sems],
    )
    merge = call(merge_body, [VM] * 3, [sds((4, 400, LANES), BF)])
    left = call(
        left_body,
        [VM] * 3,
        [sds((384, LANES), F32), sds((4, 384, LANES), BF), sds((1, LANES), F32)],
    )
    backward = call(
        backward_body,
        [SM, SM, VM, VM, ANY],
        [sds((32, 144, LANES), BF)],
        [chunk_buf, pltpu.VMEM((8, LANES, 512), F32), sems],
    )
    share_outs = [sds((LANES, LANES), F32), sds((32, LANES, LANES), BF), sds((1, LANES), F32)]
    share_first = call(functools.partial(share_body, True), [VM], share_outs)
    share = call(functools.partial(share_body, False), [VM] * 3, share_outs)

    def over_sensor(msg):
        return lax.all_to_all(msg, "sensor", 0, 0, tiled=True)

    def over_z(msg):
        return lax.all_to_all(msg, "basis", 0, 0, tiled=True, axis_index_groups=Z_GROUPS)

    (msg,) = backward(zero, slots, readings[:1536], readings[1536:], tiles)
    r, msg, bsq = share_first(over_sensor(msg))
    gathered = [over_sensor(msg)]
    bsqs = [bsq]
    asqs = []
    left_rows = lax.dynamic_slice_in_dim(readings, core[0] * 1536 + z_hi * 384, 384, 0)
    left_rows = left_rows.astype(F32)
    for sweep in range(ITERS):
        send, keep, asq = forward(core, slots, gathered[-1], tiles)
        other = lax.ppermute(send, "basis", CORE_PERM)
        (msg,) = merge(keep, other, asq)
        left_rows, msg, asq = left(over_z(msg), left_rows, bsqs[-1])
        asqs.append(asq)
        own = over_z(msg).reshape(1536, LANES)
        other = lax.ppermute(own, "basis", CORE_PERM)
        (msg,) = backward(core, slots, own, other, tiles)
        r, msg, bsq = share(over_sensor(msg), r, asq)
        bsqs.append(bsq)
        gathered.append(over_sensor(msg))
    (asq,) = call(square_body, [VM], [sds((1, LANES), F32)])(gathered[-1])
    asqs.append(lax.psum(asq, "basis"))

    betas = [jnp.sqrt(b + EPS) for b in bsqs]
    alphas = [jnp.sqrt(a + EPS) for a in asqs]
    phi_bar = betas[0]
    rho_bar = alphas[0]
    steps = []
    shifts = []
    for k in range(ITERS):
        beta, alpha = betas[k + 1], alphas[k + 1]
        rho = jnp.sqrt(rho_bar * rho_bar + beta * beta)
        cosine = rho_bar / rho
        sine = beta / rho
        theta = sine * alpha
        rho_bar = -cosine * alpha
        phi = cosine * phi_bar
        phi_bar = sine * phi_bar
        steps.append(phi / rho)
        shifts.append(theta / rho)
    s1, s2, s3 = steps
    t1, t2, t3 = shifts
    coef = jnp.concatenate(
        [
            (s1 - s2 * t1 + s3 * t2 * t1) / alphas[0],
            (s2 - s3 * t2) / alphas[1],
            s3 / alphas[2],
            -(t3 * t2 * t1) / alphas[0],
            t3 * t2 / alphas[1],
            -t3 / alphas[2],
            1.0 / alphas[3],
            jnp.zeros_like(s1),
        ],
        axis=0,
    )
    sol, search = call(
        final_body, [VM] * 5, [sds((4096, LANES), F32), sds((4096, LANES), F32)]
    )(coef, *gathered)
    return sol, search, phi_bar.reshape(LANES)


def solution(mesh):
    placed = (P("sensor", None), P("sensor", "basis", None, None, None), P("sensor", "basis", None))
    return jax.shard_map(
        per_device,
        mesh=mesh,
        in_specs=placed,
        out_specs=(P("basis", None), P("basis", None), P()),
        check_vma=False,
    )
```

```python
import functools

import jax
import jax.numpy as jnp
from jax import lax
from jax.experimental import pallas as pl
from jax.experimental.pallas import tpu as pltpu
from jax.sharding import PartitionSpec as P

CB_DEV = 8
ITERS = 3
EPS = 1e-06
LANES = 128
EXTRA = 16
TAIL = 8
VMEM_LIMIT = 24 * 1024 * 1024

BF = jnp.bfloat16
F32 = jnp.float32
Z_GROUPS = [[0, 2, 4, 6], [1, 3, 5, 7]]
CORE_PERM = [(i, i ^ 1) for i in range(8)]

VM = pl.BlockSpec(memory_space=pltpu.VMEM)
SM = pl.BlockSpec(memory_space=pltpu.SMEM)
ANY = pl.BlockSpec(memory_space=pl.ANY)


def sds(shape, dtype):
    return jax.ShapeDtypeStruct(shape, dtype)


def call(body, ins, outs, scratch=(), flops=0):
    return pl.pallas_call(
        body,
        in_specs=ins,
        out_specs=[VM] * len(outs),
        out_shape=outs,
        scratch_shapes=scratch,
        compiler_params=pltpu.CompilerParams(vmem_limit_bytes=VMEM_LIMIT),
        cost_estimate=pl.CostEstimate(
            flops=int(flops), bytes_accessed=(4 << 20) if flops else (1 << 20), transcendentals=0
        ),
    )


def pack_row(row, rows=EXTRA):
    high = row.astype(BF).astype(F32)
    low = row - high
    which = lax.broadcasted_iota(jnp.int32, (rows, LANES), 0)
    return jnp.where(which == 0, high, jnp.where(which == 1, low, 0.0))


def unpack_rows(tile):
    wide = tile.astype(F32)
    if wide.ndim == 3:
        wide = jnp.sum(wide, axis=0)
    return jnp.sum(wide, axis=0, keepdims=True)


def across(row):
    return jnp.transpose(jnp.broadcast_to(row, (LANES, LANES)))


def chunk_of(q):
    return lax.div(q, 2), pl.multiple_of(lax.rem(q, 2) * 512, 512)


def products(slot_ref, g_ref, tiles_ref, q):
    seg, top = chunk_of(q)
    acc = None
    for j in range(2):
        base = slot_ref[j, seg] * 4
        operand = jnp.concatenate([g_ref[base + t] for t in range(4)], axis=1)
        part = lax.dot_general(
            tiles_ref[seg, j, pl.ds(top, 512), :],
            operand,
            (((1,), (1,)), ((), ())),
            preferred_element_type=F32,
        )
        acc = part if acc is None else acc + part
    return acc


def squares(g_ref):
    totals = [jnp.zeros((LANES, LANES), F32) for _ in range(2)]
    for q in range(32):
        piece = g_ref[q].astype(F32)
        totals[q % 2] = totals[q % 2] + piece * piece
    return jnp.sum(jnp.transpose(totals[0] + totals[1]), axis=0, keepdims=True)


def send_body(core_ref, slot_ref, g_ref, tiles_ref, send_ref, asq_ref):
    first = 3 * (1 - core_ref[0])
    for i in range(3):
        acc = products(slot_ref, g_ref, tiles_ref, first + i)
        send_ref[i * 512 : (i + 1) * 512, :] = acc.astype(BF)
    asq = squares(g_ref)
    asq_ref[...] = asq
    send_ref[1536:1552, :] = pack_row(asq).astype(BF)


def keep_body(core_ref, slot_ref, g_ref, tiles_ref, keep_ref):
    first = 3 * core_ref[0]
    for i in range(3):
        keep_ref[i * 512 : (i + 1) * 512, :] = products(slot_ref, g_ref, tiles_ref, first + i)


def merge_body(keep_ref, recv_ref, asq_ref, msg_ref):
    tail = pack_row(asq_ref[...] + unpack_rows(recv_ref[1536:1552, :])).astype(BF)
    for z in range(4):
        part = keep_ref[z * 384 : (z + 1) * 384, :] + recv_ref[z * 384 : (z + 1) * 384, :].astype(F32)
        msg_ref[z, 0:384, :] = part.astype(BF)
        msg_ref[z, 384:400, :] = tail


def left_body(recv_ref, left_ref, bsq_ref, new_ref, msg_ref, asq_ref):
    asq = unpack_rows(recv_ref[:, 384:400, :])
    alpha = jnp.sqrt(asq + EPS)
    beta = jnp.sqrt(bsq_ref[...] + EPS)
    total = recv_ref[0, 0:384, :].astype(F32)
    for z in range(1, 4):
        total = total + recv_ref[z, 0:384, :].astype(F32)
    fresh = total * (1.0 / alpha) - (alpha / beta) * left_ref[...].astype(F32)
    new_ref[...] = fresh
    narrow = fresh.astype(BF)
    for z in range(4):
        msg_ref[z] = narrow
    asq_ref[...] = asq


def spread(slot_ref, chunk, tiles_ref, acc, q):
    seg, top = chunk_of(q)
    for j in range(2):
        acc[slot_ref[j, seg]] += lax.dot_general(
            chunk,
            tiles_ref[seg, j, pl.ds(top, 512), :],
            (((0,), (0,)), ((), ())),
            preferred_element_type=F32,
        )


def row_squares(ref):
    total = jnp.zeros((8, LANES), F32)
    for i in range(ref.shape[0] // 512):
        wide = ref[i * 512 : (i + 1) * 512, :].astype(F32)
        total = total + jnp.sum((wide * wide).reshape(64, 8, LANES), axis=0)
    return jnp.sum(total, axis=0, keepdims=True)


def write_pieces(msg_ref, tail, piece):
    for q in range(32):
        lane = (q % 4) * LANES
        msg_ref[q] = jnp.concatenate([piece(q // 4, lane), tail], axis=0).astype(BF)


def back_first_body(
    start_ref, slot_ref, rows_ref, tiles_in, msg_ref, tiles_ref, left_ref, acc, sem
):
    copy = pltpu.make_async_copy(tiles_in, tiles_ref, sem)
    copy.start()
    acc[...] = jnp.zeros_like(acc)
    left_ref[...] = rows_ref[pl.ds(pl.multiple_of(start_ref[0], 128), 384), :].astype(F32)
    tail = pack_row(row_squares(rows_ref), TAIL)
    for seg in range(3):
        for j in range(2):
            acc[slot_ref[j, seg]] += lax.dot_general(
                rows_ref[seg * 1024 : (seg + 1) * 1024, :],
                tiles_in[seg, j],
                (((0,), (0,)), ((), ())),
                preferred_element_type=F32,
            )
    write_pieces(msg_ref, tail, lambda p, lane: acc[p, :, lane : lane + LANES])
    copy.wait()


def back_own_body(core_ref, slot_ref, rows_ref, tiles_ref, acc_ref, bsq_ref):
    first = 3 * core_ref[0]
    acc_ref[...] = jnp.zeros_like(acc_ref)
    for i in range(3):
        spread(slot_ref, rows_ref[i * 512 : (i + 1) * 512, :], tiles_ref, acc_ref, first + i)
    bsq_ref[...] = row_squares(rows_ref)


def back_other_body(core_ref, slot_ref, rows_ref, acc_ref, bsq_ref, tiles_ref, msg_ref, acc):
    first = 3 * (1 - core_ref[0])
    acc[...] = acc_ref[...]
    for i in range(3):
        spread(slot_ref, rows_ref[i * 512 : (i + 1) * 512, :], tiles_ref, acc, first + i)
    tail = pack_row(row_squares(rows_ref) + bsq_ref[...], TAIL)
    write_pieces(msg_ref, tail, lambda p, lane: acc[p, :, lane : lane + LANES])


def share_body(first, recv_ref, *refs):
    if first:
        r_ref, msg_ref, bsq_ref = refs
    else:
        prev_ref, asq_ref, r_ref, msg_ref, bsq_ref = refs
    total = recv_ref[0].astype(F32)
    for q in range(1, 32):
        total = total + recv_ref[q].astype(F32)
    bsq = jnp.sum(total[LANES : LANES + TAIL, :], axis=0, keepdims=True)
    beta = jnp.sqrt(bsq + EPS)
    fresh = total[0:LANES, :] * across(1.0 / beta)
    if not first:
        alpha = jnp.sqrt(asq_ref[...] + EPS)
        fresh = fresh - across(beta / alpha) * prev_ref[...]
    r_ref[...] = fresh
    narrow = fresh.astype(BF)
    for q in range(32):
        msg_ref[q] = narrow
    bsq_ref[...] = bsq


def square_body(g_ref, msg_ref):
    tile = pack_row(squares(g_ref)).astype(BF)
    for i in range(8):
        msg_ref[i] = tile


def coef_body(b0, b1, b2, b3, a0, a1, a2, coef_ref, phi_ref):
    beta = [jnp.sqrt(b[...] + EPS) for b in (b0, b1, b2, b3)]
    alpha = [jnp.sqrt(a[...] + EPS) for a in (a0, a1, a2)]
    phi_bar, rho_bar = beta[0], alpha[0]
    steps, shifts = [], []
    for k in range(ITERS):
        rho = jnp.sqrt(rho_bar * rho_bar + beta[k + 1] * beta[k + 1])
        cosine, sine = rho_bar / rho, beta[k + 1] / rho
        steps.append(cosine * phi_bar / rho)
        phi_bar = sine * phi_bar
        if k < ITERS - 1:
            shifts.append(sine * alpha[k + 1] / rho)
            rho_bar = -cosine * alpha[k + 1]
    s1, s2, s3 = steps
    t1, t2 = shifts
    rows = [
        (s1 - s2 * t1 + s3 * t2 * t1) / alpha[0],
        (s2 - s3 * t2) / alpha[1],
        s3 / alpha[2],
        t2 * t1 / alpha[0],
        -t2 / alpha[1],
        1.0 / alpha[2],
        sine / rho,
        jnp.zeros_like(s1),
    ]
    coef_ref[...] = jnp.concatenate(rows, axis=0)
    phi_ref[...] = phi_bar


def write_out(out_hbm, stage, sems, block):
    copies = []
    for i in range(8):
        rows = pl.ds(i * 512, 512)
        for q in range(4 * i, 4 * i + 4):
            stage[q * 128 : (q + 1) * 128, :] = jnp.transpose(block(q))
        copies.append(pltpu.make_async_copy(stage.at[rows], out_hbm.at[rows], sems.at[i]))
        copies[-1].start()
    for c in copies:
        c.wait()


def solution_body(coef_ref, g0_ref, g1_ref, g2_ref, sol_hbm, stage, sems):
    rows = coef_ref[...]
    wide = [across(rows[i : i + 1, :]) for i in range(3)]

    def block(q):
        out = wide[0] * g0_ref[q].astype(F32)
        out = out + wide[1] * g1_ref[q].astype(F32)
        return out + wide[2] * g2_ref[q].astype(F32)

    write_out(sol_hbm, stage, sems, block)


def search_body(coef_ref, asq_ref, g0_ref, g1_ref, g2_ref, g3_ref, search_hbm, stage, sems):
    rows = coef_ref[...]
    alpha = jnp.sqrt(unpack_rows(asq_ref[...]) + EPS)
    shift = -alpha * rows[6:7, :]
    wide = [across(shift * rows[3 + i : 4 + i, :]) for i in range(3)] + [across(1.0 / alpha)]

    def block(q):
        out = wide[0] * g0_ref[q].astype(F32)
        out = out + wide[1] * g1_ref[q].astype(F32)
        out = out + wide[2] * g2_ref[q].astype(F32)
        return out + wide[3] * g3_ref[q].astype(F32)

    write_out(search_hbm, stage, sems, block)


def combine(body, count):
    return pl.pallas_call(
        body,
        in_specs=[VM] * count,
        out_specs=ANY,
        out_shape=sds((4096, LANES), F32),
        scratch_shapes=[pltpu.VMEM((4096, LANES), F32), pltpu.SemaphoreType.DMA((8,))],
        compiler_params=pltpu.CompilerParams(vmem_limit_bytes=VMEM_LIMIT),
        cost_estimate=pl.CostEstimate(flops=1 << 22, bytes_accessed=4 << 20, transcendentals=0),
    )


def per_device(readings, design_tiles, pattern):
    tiles = design_tiles.reshape(3, 2, 1024, 512)
    slots = jnp.transpose(pattern, (1, 2, 0)).reshape(2, 3)
    basis = lax.axis_index("basis")
    core = lax.rem(basis, 2).reshape(1).astype(jnp.int32)
    z_hi = lax.div(basis, 2)
    acc_type = sds((8, LANES, 512), F32)
    row_type = sds((1, LANES), F32)
    msg_type = sds((32, LANES + TAIL, LANES), BF)
    acc_buf = pltpu.VMEM((8, LANES, 512), F32)

    send_half = call(send_body, [SM, SM, VM, VM], [sds((1552, LANES), BF), row_type], flops=4e8)
    keep_half = call(keep_body, [SM, SM, VM, VM], [sds((1536, LANES), F32)], flops=4e8)
    merge = call(merge_body, [VM] * 3, [sds((4, 400, LANES), BF)])
    left = call(left_body, [VM] * 3, [sds((384, LANES), F32), sds((4, 384, LANES), BF), row_type])
    back_first = call(
        back_first_body,
        [SM, SM, VM, VM],
        [msg_type, sds((3, 2, 1024, 512), BF), sds((384, LANES), F32)],
        [acc_buf, pltpu.SemaphoreType.DMA(())],
        flops=8e8,
    )
    back_own = call(back_own_body, [SM, SM, VM, VM], [acc_type, row_type], flops=4e8)
    back_other = call(back_other_body, [SM, SM, VM, VM, VM, VM], [msg_type], [acc_buf], flops=4e8)
    share_outs = [sds((LANES, LANES), F32), sds((32, LANES, LANES), BF), row_type]
    share_first = call(functools.partial(share_body, True), [VM], share_outs)
    share = call(functools.partial(share_body, False), [VM] * 3, share_outs)

    def over_sensor(msg):
        return lax.all_to_all(msg, "sensor", 0, 0, tiled=True)

    def over_z(msg):
        return lax.all_to_all(msg, "basis", 0, 0, tiled=True, axis_index_groups=Z_GROUPS)

    start = core * 1536 + z_hi.astype(jnp.int32) * 384
    slots, core, start = lax.optimization_barrier((slots, core, start))
    msg, tiles, left_rows = back_first(start, slots, readings, tiles)
    r, msg, bsq = share_first(over_sensor(msg))
    gathered = [over_sensor(msg)]
    bsqs = [bsq]
    asqs = []
    for sweep in range(ITERS):
        send, asq = send_half(core, slots, gathered[-1], tiles)
        other = lax.ppermute(send, "basis", CORE_PERM)
        (keep,) = keep_half(core, slots, gathered[-1], tiles)
        (msg,) = merge(keep, other, asq)
        left_rows, msg, asq = left(over_z(msg), left_rows, bsqs[-1])
        asqs.append(asq)
        own = over_z(msg).reshape(1536, LANES)
        other = lax.ppermute(own, "basis", CORE_PERM)
        acc, own_bsq = back_own(core, slots, own, tiles)
        (msg,) = back_other(core, slots, other, acc, own_bsq, tiles)
        r, msg, bsq = share(over_sensor(msg), r, asq)
        bsqs.append(bsq)
        if sweep == ITERS - 1:
            coefs = call(coef_body, [VM] * 7, [sds((8, LANES), F32), row_type])
            coef, phi_bar = coefs(*bsqs, *asqs)
            sol = combine(solution_body, 4)(coef, *gathered)
            msg, sol, phi_bar = lax.optimization_barrier((msg, sol, phi_bar))
        gathered.append(over_sensor(msg))
    (msg,) = call(square_body, [VM], [sds((8, EXTRA, LANES), BF)])(gathered[-1])
    msg = lax.all_to_all(msg, "basis", 0, 0, tiled=True)
    search = combine(search_body, 6)(coef, msg, *gathered)
    return sol, search, phi_bar.reshape(LANES)


def solution(mesh):
    placed = (P("sensor", None), P("sensor", "basis", None, None, None), P("sensor", "basis", None))
    return jax.shard_map(
        per_device,
        mesh=mesh,
        in_specs=placed,
        out_specs=(P("basis", None), P("basis", None), P()),
        check_vma=False,
    )
```

```python
import functools

import jax
import jax.numpy as jnp
from jax import lax
from jax.experimental import pallas as pl
from jax.experimental.pallas import tpu as pltpu
from jax.sharding import PartitionSpec as P

CB_DEV = 8
ITERS = 3
EPS = 1e-06
LANES = 128
EXTRA = 16
TAIL = 8
VMEM_LIMIT = 24 * 1024 * 1024

BF = jnp.bfloat16
F32 = jnp.float32
Z_GROUPS = [[6, 4, 2, 0], [7, 5, 3, 1]]
S_GROUPS = [[(y * 4 + x) * 2 + z for z in range(2) for x in range(4) for y in range(4)]]
CORE_PERM = [(i, i ^ 1) for i in range(8)]

VM = pl.BlockSpec(memory_space=pltpu.VMEM)
SM = pl.BlockSpec(memory_space=pltpu.SMEM)
ANY = pl.BlockSpec(memory_space=pl.ANY)


def sds(shape, dtype):
    return jax.ShapeDtypeStruct(shape, dtype)


def call(body, ins, outs, scratch=(), flops=0):
    return pl.pallas_call(
        body,
        in_specs=ins,
        out_specs=[VM] * len(outs),
        out_shape=outs,
        scratch_shapes=scratch,
        compiler_params=pltpu.CompilerParams(vmem_limit_bytes=VMEM_LIMIT),
        cost_estimate=pl.CostEstimate(
            flops=int(flops), bytes_accessed=(4 << 20) if flops else (1 << 20), transcendentals=0
        ),
    )


def pack_row(row, rows=EXTRA):
    high = row.astype(BF).astype(F32)
    low = row - high
    which = lax.broadcasted_iota(jnp.int32, (rows, LANES), 0)
    return jnp.where(which == 0, high, jnp.where(which == 1, low, 0.0))


def unpack_rows(tile):
    wide = tile.astype(F32)
    if wide.ndim == 3:
        wide = jnp.sum(wide, axis=0)
    return jnp.sum(wide, axis=0, keepdims=True)


def across(row):
    return jnp.transpose(jnp.broadcast_to(row, (LANES, LANES)))


def chunk_of(q):
    return lax.div(q, 2), pl.multiple_of(lax.rem(q, 2) * 512, 512)


def products(slot_ref, g_ref, tiles_ref, q):
    seg, top = chunk_of(q)
    acc = None
    for j in range(2):
        base = slot_ref[j, seg] * 4
        operand = jnp.concatenate([g_ref[base + t] for t in range(4)], axis=1)
        part = lax.dot_general(
            tiles_ref[seg, j, pl.ds(top, 512), :],
            operand,
            (((1,), (1,)), ((), ())),
            preferred_element_type=F32,
        )
        acc = part if acc is None else acc + part
    return acc


def squares(g_ref):
    totals = [jnp.zeros((LANES, LANES), F32) for _ in range(2)]
    for q in range(32):
        piece = g_ref[q].astype(F32)
        totals[q % 2] = totals[q % 2] + piece * piece
    return jnp.sum(jnp.transpose(totals[0] + totals[1]), axis=0, keepdims=True)


def send_body(core_ref, slot_ref, g_ref, tiles_ref, send_ref, asq_ref):
    first = 3 * (1 - core_ref[0])
    for i in range(3):
        acc = products(slot_ref, g_ref, tiles_ref, first + i)
        send_ref[i * 512 : (i + 1) * 512, :] = acc.astype(BF)
    asq = squares(g_ref)
    asq_ref[...] = asq
    send_ref[1536:1552, :] = pack_row(asq).astype(BF)


def keep_body(core_ref, slot_ref, g_ref, tiles_ref, keep_ref):
    first = 3 * core_ref[0]
    for i in range(3):
        keep_ref[i * 512 : (i + 1) * 512, :] = products(slot_ref, g_ref, tiles_ref, first + i)


def merge_body(keep_ref, recv_ref, asq_ref, msg_ref):
    tail = pack_row(asq_ref[...] + unpack_rows(recv_ref[1536:1552, :])).astype(BF)
    for z in range(4):
        part = keep_ref[z * 384 : (z + 1) * 384, :] + recv_ref[z * 384 : (z + 1) * 384, :].astype(F32)
        msg_ref[z, 0:384, :] = part.astype(BF)
        msg_ref[z, 384:400, :] = tail


def left_body(recv_ref, left_ref, bsq_ref, msg_ref, asq_ref, new_ref=None):
    asq = unpack_rows(recv_ref[:, 384:400, :])
    alpha = jnp.sqrt(asq + EPS)
    beta = jnp.sqrt(bsq_ref[...] + EPS)
    total = recv_ref[0, 0:384, :].astype(F32)
    for z in range(1, 4):
        total = total + recv_ref[z, 0:384, :].astype(F32)
    fresh = total * (1.0 / alpha) - (alpha / beta) * left_ref[...].astype(F32)
    if new_ref is not None:
        new_ref[...] = fresh
    narrow = fresh.astype(BF)
    for z in range(4):
        msg_ref[z] = narrow
    asq_ref[...] = asq


def spread(slot_ref, chunk, tiles_ref, acc, q):
    seg, top = chunk_of(q)
    for j in range(2):
        acc[slot_ref[j, seg]] += lax.dot_general(
            chunk,
            tiles_ref[seg, j, pl.ds(top, 512), :],
            (((0,), (0,)), ((), ())),
            preferred_element_type=F32,
        )


def row_squares(ref):
    total = jnp.zeros((8, LANES), F32)
    for i in range(ref.shape[0] // 512):
        wide = ref[i * 512 : (i + 1) * 512, :].astype(F32)
        total = total + jnp.sum((wide * wide).reshape(64, 8, LANES), axis=0)
    return jnp.sum(total, axis=0, keepdims=True)


def write_pieces(msg_ref, tail, piece):
    for q in range(32):
        lane = (q % 4) * LANES
        msg_ref[q] = jnp.concatenate([piece(q // 4, lane), tail], axis=0).astype(BF)


def back_first_body(
    start_ref, slot_ref, rows_ref, tiles_in, msg_ref, tiles_ref, left_ref, acc, sem
):
    copy = pltpu.make_async_copy(tiles_in, tiles_ref, sem)
    copy.start()
    acc[...] = jnp.zeros_like(acc)
    left_ref[...] = rows_ref[pl.ds(pl.multiple_of(start_ref[0], 128), 384), :].astype(F32)
    tail = pack_row(row_squares(rows_ref), TAIL)
    for seg in range(3):
        for j in range(2):
            acc[slot_ref[j, seg]] += lax.dot_general(
                rows_ref[seg * 1024 : (seg + 1) * 1024, :],
                tiles_in[seg, j],
                (((0,), (0,)), ((), ())),
                preferred_element_type=F32,
            )
    write_pieces(msg_ref, tail, lambda p, lane: acc[p, :, lane : lane + LANES])
    copy.wait()


def back_own_body(core_ref, slot_ref, rows_ref, tiles_ref, acc_ref, bsq_ref):
    first = 3 * core_ref[0]
    acc_ref[...] = jnp.zeros_like(acc_ref)
    for i in range(3):
        spread(slot_ref, rows_ref[i * 512 : (i + 1) * 512, :], tiles_ref, acc_ref, first + i)
    bsq_ref[...] = row_squares(rows_ref)


def back_other_body(core_ref, slot_ref, rows_ref, acc_ref, bsq_ref, tiles_ref, msg_ref, acc):
    first = 3 * (1 - core_ref[0])
    acc[...] = acc_ref[...]
    for i in range(3):
        spread(slot_ref, rows_ref[i * 512 : (i + 1) * 512, :], tiles_ref, acc, first + i)
    tail = pack_row(row_squares(rows_ref) + bsq_ref[...], TAIL)
    write_pieces(msg_ref, tail, lambda p, lane: acc[p, :, lane : lane + LANES])


def share_body(first, last, recv_ref, *refs):
    if not first:
        prev_ref, asq_ref = refs[:2]
        refs = refs[2:]
    msg_ref, bsq_ref = refs[:2]
    total = recv_ref[0].astype(F32)
    for q in range(1, 32):
        total = total + recv_ref[q].astype(F32)
    bsq = jnp.sum(total[LANES : LANES + TAIL, :], axis=0, keepdims=True)
    beta = jnp.sqrt(bsq + EPS)
    fresh = total[0:LANES, :] * across(1.0 / beta)
    if not first:
        alpha = jnp.sqrt(asq_ref[...] + EPS)
        fresh = fresh - across(beta / alpha) * prev_ref[...]
    if not last:
        refs[2][...] = fresh
    narrow = fresh.astype(BF)
    for q in range(32):
        msg_ref[q] = narrow
    bsq_ref[...] = bsq


def square_body(g_ref, msg_ref):
    tile = pack_row(squares(g_ref)).astype(BF)
    for i in range(8):
        msg_ref[i] = tile


def coefficients(b0, b1, b2, b3, a0, a1, a2):
    beta = [jnp.sqrt(b[...] + EPS) for b in (b0, b1, b2, b3)]
    alpha = [jnp.sqrt(a[...] + EPS) for a in (a0, a1, a2)]
    phi_bar, rho_bar = beta[0], alpha[0]
    steps, shifts = [], []
    for k in range(ITERS):
        rho = jnp.sqrt(rho_bar * rho_bar + beta[k + 1] * beta[k + 1])
        cosine, sine = rho_bar / rho, beta[k + 1] / rho
        steps.append(cosine * phi_bar / rho)
        phi_bar = sine * phi_bar
        if k < ITERS - 1:
            shifts.append(sine * alpha[k + 1] / rho)
            rho_bar = -cosine * alpha[k + 1]
    s1, s2, s3 = steps
    t1, t2 = shifts
    rows = [
        (s1 - s2 * t1 + s3 * t2 * t1) / alpha[0],
        (s2 - s3 * t2) / alpha[1],
        s3 / alpha[2],
        t2 * t1 / alpha[0],
        -t2 / alpha[1],
        1.0 / alpha[2],
        sine / rho,
        jnp.zeros_like(s1),
    ]
    return jnp.concatenate(rows, axis=0), phi_bar


def write_out(out_hbm, stage, sems, block):
    copies = []
    for i in range(8):
        rows = pl.ds(i * 512, 512)
        for q in range(4 * i, 4 * i + 4):
            stage[q * 128 : (q + 1) * 128, :] = jnp.transpose(block(q))
        copies.append(pltpu.make_async_copy(stage.at[rows], out_hbm.at[rows], sems.at[i]))
        copies[-1].start()
    for c in copies:
        c.wait()


def solution_body(*refs):
    g0_ref, g1_ref, g2_ref, sol_hbm, coef_ref, phi_ref, stage, sems = refs[7:]
    rows, phi_bar = coefficients(*refs[:7])
    coef_ref[...] = rows
    phi_ref[...] = phi_bar
    wide = [across(rows[i : i + 1, :]) for i in range(3)]

    def block(q):
        out = wide[0] * g0_ref[q].astype(F32)
        out = out + wide[1] * g1_ref[q].astype(F32)
        return out + wide[2] * g2_ref[q].astype(F32)

    write_out(sol_hbm, stage, sems, block)


def search_body(coef_ref, asq_ref, g0_ref, g1_ref, g2_ref, g3_ref, search_hbm, stage, sems):
    rows = coef_ref[...]
    alpha = jnp.sqrt(unpack_rows(asq_ref[...]) + EPS)
    shift = -alpha * rows[6:7, :]
    wide = [across(shift * rows[3 + i : 4 + i, :]) for i in range(3)] + [across(1.0 / alpha)]

    def block(q):
        out = wide[0] * g0_ref[q].astype(F32)
        out = out + wide[1] * g1_ref[q].astype(F32)
        out = out + wide[2] * g2_ref[q].astype(F32)
        return out + wide[3] * g3_ref[q].astype(F32)

    write_out(search_hbm, stage, sems, block)


def combine(body, count, smalls=()):
    return pl.pallas_call(
        body,
        in_specs=[VM] * count,
        out_specs=[ANY] + [VM] * len(smalls),
        out_shape=[sds((4096, LANES), F32)] + list(smalls),
        scratch_shapes=[pltpu.VMEM((4096, LANES), F32), pltpu.SemaphoreType.DMA((8,))],
        compiler_params=pltpu.CompilerParams(vmem_limit_bytes=VMEM_LIMIT),
        cost_estimate=pl.CostEstimate(flops=1 << 22, bytes_accessed=4 << 20, transcendentals=0),
    )


def per_device(readings, design_tiles, pattern):
    tiles = design_tiles.reshape(3, 2, 1024, 512)
    slots = jnp.transpose(pattern, (1, 2, 0)).reshape(2, 3)
    basis = lax.axis_index("basis")
    core = lax.rem(basis, 2).reshape(1).astype(jnp.int32)
    z_hi = lax.div(basis, 2)
    acc_type = sds((8, LANES, 512), F32)
    row_type = sds((1, LANES), F32)
    msg_type = sds((32, LANES + TAIL, LANES), BF)
    acc_buf = pltpu.VMEM((8, LANES, 512), F32)

    send_half = call(send_body, [SM, SM, VM, VM], [sds((1552, LANES), BF), row_type], flops=4e8)
    keep_half = call(keep_body, [SM, SM, VM, VM], [sds((1536, LANES), F32)], flops=4e8)
    merge = call(merge_body, [VM] * 3, [sds((4, 400, LANES), BF)])
    left_outs = [sds((4, 384, LANES), BF), row_type, sds((384, LANES), F32)]
    left = call(left_body, [VM] * 3, left_outs)
    left_last = call(left_body, [VM] * 3, left_outs[:2])
    back_first = call(
        back_first_body,
        [SM, SM, VM, VM],
        [msg_type, sds((3, 2, 1024, 512), BF), sds((384, LANES), F32)],
        [acc_buf, pltpu.SemaphoreType.DMA(())],
        flops=8e8,
    )
    back_own = call(back_own_body, [SM, SM, VM, VM], [acc_type, row_type], flops=4e8)
    back_other = call(back_other_body, [SM, SM, VM, VM, VM, VM], [msg_type], [acc_buf], flops=4e8)
    share_outs = [sds((32, LANES, LANES), BF), row_type, sds((LANES, LANES), F32)]
    share_first = call(functools.partial(share_body, True, False), [VM], share_outs)
    share = call(functools.partial(share_body, False, False), [VM] * 3, share_outs)
    share_last = call(functools.partial(share_body, False, True), [VM] * 3, share_outs[:2])

    solve = combine(solution_body, 10, [sds((8, LANES), F32), row_type])

    def over_sensor(msg):
        return lax.all_to_all(msg, "sensor", 0, 0, tiled=True, axis_index_groups=S_GROUPS)

    def over_z(msg):
        return lax.all_to_all(msg, "basis", 0, 0, tiled=True, axis_index_groups=Z_GROUPS)

    start = core * 1536 + (3 - z_hi.astype(jnp.int32)) * 384
    slots, core, start = lax.optimization_barrier((slots, core, start))
    msg, tiles, left_rows = back_first(start, slots, readings, tiles)
    msg, bsq, r = share_first(over_sensor(msg))
    gathered = [over_sensor(msg)]
    bsqs = [bsq]
    asqs = []
    for sweep in range(ITERS):
        last = sweep == ITERS - 1
        send, asq = send_half(core, slots, gathered[-1], tiles)
        other = lax.ppermute(send, "basis", CORE_PERM)
        (keep,) = keep_half(core, slots, gathered[-1], tiles)
        (msg,) = merge(keep, other, asq)
        if last:
            msg, asq = left_last(over_z(msg), left_rows, bsqs[-1])
        else:
            msg, asq, left_rows = left(over_z(msg), left_rows, bsqs[-1])
        asqs.append(asq)
        own = over_z(msg).reshape(1536, LANES)
        other = lax.ppermute(own, "basis", CORE_PERM)
        acc, own_bsq = back_own(core, slots, own, tiles)
        (msg,) = back_other(core, slots, other, acc, own_bsq, tiles)
        if last:
            msg, bsq = share_last(over_sensor(msg), r, asq)
        else:
            msg, bsq, r = share(over_sensor(msg), r, asq)
        bsqs.append(bsq)
        if last:
            sol, coef, phi_bar = solve(*bsqs, *asqs, *gathered)
            msg, sol, phi_bar = lax.optimization_barrier((msg, sol, phi_bar))
        gathered.append(over_sensor(msg))
    (msg,) = call(square_body, [VM], [sds((8, EXTRA, LANES), BF)])(gathered[-1])
    msg = lax.all_to_all(msg, "basis", 0, 0, tiled=True)
    (search,) = combine(search_body, 6)(coef, msg, *gathered)
    return sol, search, phi_bar.reshape(LANES)


def solution(mesh):
    placed = (P("sensor", None), P("sensor", "basis", None, None, None), P("sensor", "basis", None))
    return jax.shard_map(
        per_device,
        mesh=mesh,
        in_specs=placed,
        out_specs=(P("basis", None), P("basis", None), P()),
        check_vma=False,
    )
```

```python
import functools

import jax
import jax.numpy as jnp
from jax import lax
from jax.experimental import pallas as pl
from jax.experimental.pallas import tpu as pltpu
from jax.sharding import PartitionSpec as P

CB_DEV = 8
ITERS = 3
EPS = 1e-06
LANES = 128
EXTRA = 16
TAIL = 8
VMEM_LIMIT = 24 * 1024 * 1024

BF = jnp.bfloat16
F32 = jnp.float32
Z_GROUPS = [[6, 4, 2, 0], [7, 5, 3, 1]]
S_GROUPS = [[(y * 4 + x) * 2 + z for z in range(2) for x in range(4) for y in (3, 2, 1, 0)]]
CORE_PERM = [(i, i ^ 1) for i in range(8)]

VM = pl.BlockSpec(memory_space=pltpu.VMEM)
SM = pl.BlockSpec(memory_space=pltpu.SMEM)
ANY = pl.BlockSpec(memory_space=pl.ANY)


def sds(shape, dtype):
    return jax.ShapeDtypeStruct(shape, dtype)


def call(body, ins, outs, scratch=(), flops=0):
    return pl.pallas_call(
        body,
        in_specs=ins,
        out_specs=[VM] * len(outs),
        out_shape=outs,
        scratch_shapes=scratch,
        compiler_params=pltpu.CompilerParams(vmem_limit_bytes=VMEM_LIMIT),
        cost_estimate=pl.CostEstimate(
            flops=int(flops), bytes_accessed=(4 << 20) if flops else (1 << 20), transcendentals=0
        ),
    )


def pack_row(row, rows=EXTRA):
    high = row.astype(BF).astype(F32)
    low = row - high
    which = lax.broadcasted_iota(jnp.int32, (rows, LANES), 0)
    return jnp.where(which == 0, high, jnp.where(which == 1, low, 0.0))


def unpack_rows(tile):
    wide = tile.astype(F32)
    if wide.ndim == 3:
        wide = jnp.sum(wide, axis=0)
    return jnp.sum(wide, axis=0, keepdims=True)


def across(row):
    return jnp.transpose(jnp.broadcast_to(row, (LANES, LANES)))


def parts_of(half):
    middle = pl.multiple_of(half * 512, 512)
    return (
        (2 * half, 0, 1024, middle),
        (1, middle, 512, pl.multiple_of((1 - half) * 1024, 512)),
    )


def products(slot_ref, g_ref, tiles_ref, seg, top, rows):
    acc = None
    for j in range(2):
        part = jnp.dot(
            tiles_ref[seg, j, pl.ds(top, rows), :],
            g_ref[slot_ref[j, seg]],
            preferred_element_type=F32,
        )
        acc = part if acc is None else acc + part
    return acc


def column_squares(g_ref):
    total = jnp.zeros((8, LANES), F32)
    for p in range(8):
        wide = g_ref[p].astype(F32)
        total = total + jnp.sum((wide * wide).reshape(64, 8, LANES), axis=0)
    return jnp.sum(total, axis=0, keepdims=True)


def send_body(core_ref, slot_ref, g_ref, tiles_ref, send_ref, asq_ref):
    for seg, top, rows, at in parts_of(1 - core_ref[0]):
        acc = products(slot_ref, g_ref, tiles_ref, seg, top, rows)
        send_ref[pl.ds(at, rows), :] = acc.astype(BF)
    asq = column_squares(g_ref)
    asq_ref[...] = asq
    send_ref[1536:1552, :] = pack_row(asq).astype(BF)


def keep_body(core_ref, slot_ref, g_ref, tiles_ref, keep_ref):
    for seg, top, rows, at in parts_of(core_ref[0]):
        keep_ref[pl.ds(at, rows), :] = products(slot_ref, g_ref, tiles_ref, seg, top, rows)


def merge_body(keep_ref, recv_ref, asq_ref, msg_ref):
    tail = pack_row(asq_ref[...] + unpack_rows(recv_ref[1536:1552, :])).astype(BF)
    for z in range(4):
        part = keep_ref[z * 384 : (z + 1) * 384, :] + recv_ref[z * 384 : (z + 1) * 384, :].astype(F32)
        msg_ref[z, 0:384, :] = part.astype(BF)
        msg_ref[z, 384:400, :] = tail


def left_body(recv_ref, left_ref, bsq_ref, msg_ref, asq_ref, new_ref=None):
    asq = unpack_rows(recv_ref[:, 384:400, :])
    alpha = jnp.sqrt(asq + EPS)
    beta = jnp.sqrt(bsq_ref[...] + EPS)
    total = recv_ref[0, 0:384, :].astype(F32)
    for z in range(1, 4):
        total = total + recv_ref[z, 0:384, :].astype(F32)
    fresh = total * (1.0 / alpha) - (alpha / beta) * left_ref[...].astype(F32)
    if new_ref is not None:
        new_ref[...] = fresh
    narrow = fresh.astype(BF)
    for z in range(4):
        msg_ref[z] = narrow
    asq_ref[...] = asq


def spread(slot_ref, rows_ref, tiles_ref, acc, half):
    for seg, top, rows, at in parts_of(half):
        chunk = rows_ref[pl.ds(at, rows), :]
        for j in range(2):
            acc[slot_ref[j, seg]] += lax.dot_general(
                chunk,
                tiles_ref[seg, j, pl.ds(top, rows), :],
                (((0,), (0,)), ((), ())),
                preferred_element_type=F32,
            )


def row_squares(ref):
    total = jnp.zeros((8, LANES), F32)
    for i in range(ref.shape[0] // 512):
        wide = ref[i * 512 : (i + 1) * 512, :].astype(F32)
        total = total + jnp.sum((wide * wide).reshape(64, 8, LANES), axis=0)
    return jnp.sum(total, axis=0, keepdims=True)


def write_pieces(msg_ref, tail, piece):
    for q in range(32):
        lane = (q % 4) * LANES
        msg_ref[q] = jnp.concatenate([piece(q // 4, lane), tail], axis=0).astype(BF)


def back_first_body(
    start_ref, slot_ref, rows_ref, tiles_in, msg_ref, tiles_ref, left_ref, acc, sem
):
    copy = pltpu.make_async_copy(tiles_in, tiles_ref, sem)
    copy.start()
    acc[...] = jnp.zeros_like(acc)
    left_ref[...] = rows_ref[pl.ds(pl.multiple_of(start_ref[0], 128), 384), :].astype(F32)
    tail = pack_row(row_squares(rows_ref), TAIL)
    for seg in range(3):
        for j in range(2):
            acc[slot_ref[j, seg]] += lax.dot_general(
                rows_ref[seg * 1024 : (seg + 1) * 1024, :],
                tiles_in[seg, j],
                (((0,), (0,)), ((), ())),
                preferred_element_type=F32,
            )
    write_pieces(msg_ref, tail, lambda p, lane: acc[p, :, lane : lane + LANES])
    copy.wait()


def back_own_body(core_ref, slot_ref, rows_ref, tiles_ref, acc_ref, bsq_ref):
    acc_ref[...] = jnp.zeros_like(acc_ref)
    spread(slot_ref, rows_ref, tiles_ref, acc_ref, core_ref[0])
    bsq_ref[...] = row_squares(rows_ref)


def back_other_body(core_ref, slot_ref, rows_ref, acc_ref, bsq_ref, tiles_ref, msg_ref, acc):
    acc[...] = acc_ref[...]
    spread(slot_ref, rows_ref, tiles_ref, acc, 1 - core_ref[0])
    tail = pack_row(row_squares(rows_ref) + bsq_ref[...], TAIL)
    write_pieces(msg_ref, tail, lambda p, lane: acc[p, :, lane : lane + LANES])


def share_body(first, last, recv_ref, *refs):
    if not first:
        prev_ref, asq_ref = refs[:2]
        refs = refs[2:]
    msg_ref, bsq_ref = refs[:2]
    total = recv_ref[0].astype(F32)
    for q in range(1, 32):
        total = total + recv_ref[q].astype(F32)
    bsq = jnp.sum(total[LANES : LANES + TAIL, :], axis=0, keepdims=True)
    beta = jnp.sqrt(bsq + EPS)
    fresh = total[0:LANES, :] * across(1.0 / beta)
    if not first:
        alpha = jnp.sqrt(asq_ref[...] + EPS)
        fresh = fresh - across(beta / alpha) * prev_ref[...]
    if not last:
        refs[2][...] = fresh
    narrow = jnp.transpose(fresh).astype(BF)
    for q in range(32):
        msg_ref[q] = narrow
    bsq_ref[...] = bsq


def square_body(g_ref, msg_ref):
    tile = pack_row(column_squares(g_ref)).astype(BF)
    for i in range(8):
        msg_ref[i] = tile


def coefficients(b0, b1, b2, b3, a0, a1, a2):
    beta = [jnp.sqrt(b[...] + EPS) for b in (b0, b1, b2, b3)]
    alpha = [jnp.sqrt(a[...] + EPS) for a in (a0, a1, a2)]
    phi_bar, rho_bar = beta[0], alpha[0]
    steps, shifts = [], []
    for k in range(ITERS):
        rho = jnp.sqrt(rho_bar * rho_bar + beta[k + 1] * beta[k + 1])
        cosine, sine = rho_bar / rho, beta[k + 1] / rho
        steps.append(cosine * phi_bar / rho)
        phi_bar = sine * phi_bar
        if k < ITERS - 1:
            shifts.append(sine * alpha[k + 1] / rho)
            rho_bar = -cosine * alpha[k + 1]
    s1, s2, s3 = steps
    t1, t2 = shifts
    rows = [
        (s1 - s2 * t1 + s3 * t2 * t1) / alpha[0],
        (s2 - s3 * t2) / alpha[1],
        s3 / alpha[2],
        t2 * t1 / alpha[0],
        -t2 / alpha[1],
        1.0 / alpha[2],
        sine / rho,
        jnp.zeros_like(s1),
    ]
    return jnp.concatenate(rows, axis=0), phi_bar


def final_body(*refs):
    asq_ref = refs[7]
    gathered = refs[8:12]
    sol_hbm, search_hbm, phi_ref, stage, sems = refs[12:]
    rows, phi_bar = coefficients(*refs[:7])
    phi_ref[...] = phi_bar
    alpha = jnp.sqrt(unpack_rows(asq_ref[...]) + EPS)
    older = -alpha * rows[6:7] * rows[3:6]
    newest = 1.0 / alpha
    copies = []
    for p in range(8):
        at = pl.ds(p * 512, 512)
        g0, g1, g2, g3 = [ref[p].astype(F32) for ref in gathered]
        stage[0, at, :] = rows[0:1] * g0 + rows[1:2] * g1 + rows[2:3] * g2
        stage[1, at, :] = older[0:1] * g0 + older[1:2] * g1 + older[2:3] * g2 + newest * g3
        for i, out in enumerate((sol_hbm, search_hbm)):
            copies.append(pltpu.make_async_copy(stage.at[i, at], out.at[at], sems.at[i, p]))
            copies[-1].start()
    for c in copies:
        c.wait()


def per_device(readings, design_tiles, pattern):
    tiles = design_tiles.reshape(3, 2, 1024, 512)
    slots = jnp.transpose(pattern, (1, 2, 0)).reshape(2, 3)
    basis = lax.axis_index("basis")
    core = lax.rem(basis, 2).reshape(1).astype(jnp.int32)
    z_hi = lax.div(basis, 2)
    acc_type = sds((8, LANES, 512), F32)
    row_type = sds((1, LANES), F32)
    msg_type = sds((32, LANES + TAIL, LANES), BF)
    acc_buf = pltpu.VMEM((8, LANES, 512), F32)

    send_half = call(send_body, [SM, SM, VM, VM], [sds((1552, LANES), BF), row_type], flops=4e8)
    keep_half = call(keep_body, [SM, SM, VM, VM], [sds((1536, LANES), F32)], flops=4e8)
    merge = call(merge_body, [VM] * 3, [sds((4, 400, LANES), BF)])
    left_outs = [sds((4, 384, LANES), BF), row_type, sds((384, LANES), F32)]
    left = call(left_body, [VM] * 3, left_outs)
    left_last = call(left_body, [VM] * 3, left_outs[:2])
    back_first = call(
        back_first_body,
        [SM, SM, VM, VM],
        [msg_type, sds((3, 2, 1024, 512), BF), sds((384, LANES), F32)],
        [acc_buf, pltpu.SemaphoreType.DMA(())],
        flops=8e8,
    )
    back_own = call(back_own_body, [SM, SM, VM, VM], [acc_type, row_type], flops=4e8)
    back_other = call(back_other_body, [SM, SM, VM, VM, VM, VM], [msg_type], [acc_buf], flops=4e8)
    share_outs = [sds((32, LANES, LANES), BF), row_type, sds((LANES, LANES), F32)]
    share_first = call(functools.partial(share_body, True, False), [VM], share_outs)
    share = call(functools.partial(share_body, False, False), [VM] * 3, share_outs)
    share_last = call(functools.partial(share_body, False, True), [VM] * 3, share_outs[:2])

    finish = pl.pallas_call(
        final_body,
        in_specs=[VM] * 12,
        out_specs=[ANY, ANY, VM],
        out_shape=[sds((4096, LANES), F32), sds((4096, LANES), F32), row_type],
        scratch_shapes=[pltpu.VMEM((2, 4096, LANES), F32), pltpu.SemaphoreType.DMA((2, 8))],
        compiler_params=pltpu.CompilerParams(vmem_limit_bytes=VMEM_LIMIT),
    )

    def gather(msg):
        return over_sensor(msg).reshape(8, 512, LANES)

    def over_sensor(msg):
        return lax.all_to_all(msg, "sensor", 0, 0, tiled=True, axis_index_groups=S_GROUPS)

    def over_z(msg):
        return lax.all_to_all(msg, "basis", 0, 0, tiled=True, axis_index_groups=Z_GROUPS)

    start = core * 1536 + (3 - z_hi.astype(jnp.int32)) * 384
    slots, core, start = lax.optimization_barrier((slots, core, start))
    msg, tiles, left_rows = back_first(start, slots, readings, tiles)
    msg, bsq, r = share_first(over_sensor(msg))
    gathered = [gather(msg)]
    bsqs = [bsq]
    asqs = []
    for sweep in range(ITERS):
        last = sweep == ITERS - 1
        send, asq = send_half(core, slots, gathered[-1], tiles)
        other = lax.ppermute(send, "basis", CORE_PERM)
        (keep,) = keep_half(core, slots, gathered[-1], tiles)
        (msg,) = merge(keep, other, asq)
        if last:
            msg, asq = left_last(over_z(msg), left_rows, bsqs[-1])
        else:
            msg, asq, left_rows = left(over_z(msg), left_rows, bsqs[-1])
        asqs.append(asq)
        own = over_z(msg).reshape(1536, LANES)
        other = lax.ppermute(own, "basis", CORE_PERM)
        acc, own_bsq = back_own(core, slots, own, tiles)
        (msg,) = back_other(core, slots, other, acc, own_bsq, tiles)
        if last:
            msg, bsq = share_last(over_sensor(msg), r, asq)
        else:
            msg, bsq, r = share(over_sensor(msg), r, asq)
        bsqs.append(bsq)
        gathered.append(gather(msg))
    (msg,) = call(square_body, [VM], [sds((8, EXTRA, LANES), BF)])(gathered[-1])
    msg = lax.all_to_all(msg, "basis", 0, 0, tiled=True)
    sol, search, phi_bar = finish(*bsqs, *asqs, msg, *gathered)
    return sol, search, phi_bar.reshape(LANES)


def solution(mesh):
    placed = (P("sensor", None), P("sensor", "basis", None, None, None), P("sensor", "basis", None))
    return jax.shard_map(
        per_device,
        mesh=mesh,
        in_specs=placed,
        out_specs=(P("basis", None), P("basis", None), P()),
        check_vma=False,
    )
```

```python
import functools

import jax
import jax.numpy as jnp
from jax import lax
from jax.experimental import pallas as pl
from jax.experimental.pallas import tpu as pltpu
from jax.sharding import PartitionSpec as P

CB_DEV = 8
ITERS = 3
EPS = 1e-06
LANES = 128
EXTRA = 16
TAIL = 8
VMEM_LIMIT = 24 * 1024 * 1024

BF = jnp.bfloat16
F32 = jnp.float32
Z_GROUPS = [[6, 4, 2, 0], [7, 5, 3, 1]]
S_GROUPS = [[(y * 4 + x) * 2 + z for z in range(2) for x in (3, 2, 1, 0) for y in (3, 2, 1, 0)]]
CORE_PERM = [(i, i ^ 1) for i in range(8)]

VM = pl.BlockSpec(memory_space=pltpu.VMEM)
SM = pl.BlockSpec(memory_space=pltpu.SMEM)
ANY = pl.BlockSpec(memory_space=pl.ANY)


def sds(shape, dtype):
    return jax.ShapeDtypeStruct(shape, dtype)


def call(body, ins, outs, scratch=(), flops=0, aliases=None):
    return pl.pallas_call(
        body,
        in_specs=ins,
        out_specs=[VM] * len(outs),
        out_shape=outs,
        scratch_shapes=scratch,
        input_output_aliases=aliases or {},
        compiler_params=pltpu.CompilerParams(vmem_limit_bytes=VMEM_LIMIT),
        cost_estimate=pl.CostEstimate(
            flops=int(flops), bytes_accessed=(4 << 20) if flops else (1 << 20), transcendentals=0
        ),
    )


def pack_row(row, rows=EXTRA):
    high = row.astype(BF).astype(F32)
    low = row - high
    which = lax.broadcasted_iota(jnp.int32, (rows, LANES), 0)
    return jnp.where(which == 0, high, jnp.where(which == 1, low, 0.0))


def unpack_rows(tile):
    wide = tile.astype(F32)
    if wide.ndim == 3:
        wide = jnp.sum(wide, axis=0)
    return jnp.sum(wide, axis=0, keepdims=True)


def across(row):
    return jnp.transpose(jnp.broadcast_to(row, (LANES, LANES)))


def parts_of(half):
    middle = pl.multiple_of(half * 512, 512)
    return (
        (2 * half, 0, 1024, middle),
        (1, middle, 512, pl.multiple_of((1 - half) * 1024, 512)),
    )


def products(slot_ref, g_ref, tiles_ref, seg, top, rows):
    acc = None
    for j in range(2):
        part = jnp.dot(
            tiles_ref[seg, j, pl.ds(top, rows), :],
            g_ref[slot_ref[j, seg]],
            preferred_element_type=F32,
        )
        acc = part if acc is None else acc + part
    return acc


def column_squares(g_ref):
    total = jnp.zeros((8, LANES), F32)
    for p in range(8):
        wide = g_ref[p].astype(F32)
        total = total + jnp.sum((wide * wide).reshape(64, 8, LANES), axis=0)
    return jnp.sum(total, axis=0, keepdims=True)


def send_body(core_ref, slot_ref, g_ref, tiles_ref, send_ref, asq_ref):
    for seg, top, rows, at in parts_of(1 - core_ref[0]):
        acc = products(slot_ref, g_ref, tiles_ref, seg, top, rows)
        send_ref[pl.ds(at, rows), :] = acc.astype(BF)
    asq = column_squares(g_ref)
    asq_ref[...] = asq
    send_ref[1536:1552, :] = pack_row(asq).astype(BF)


def keep_body(core_ref, slot_ref, g_ref, tiles_ref, keep_ref):
    for seg, top, rows, at in parts_of(core_ref[0]):
        keep_ref[pl.ds(at, rows), :] = products(slot_ref, g_ref, tiles_ref, seg, top, rows)


def merge_body(keep_ref, recv_ref, asq_ref, msg_ref):
    tail = pack_row(asq_ref[...] + unpack_rows(recv_ref[1536:1552, :])).astype(BF)
    for z in range(4):
        part = keep_ref[z * 384 : (z + 1) * 384, :] + recv_ref[z * 384 : (z + 1) * 384, :].astype(F32)
        msg_ref[z, 0:384, :] = part.astype(BF)
        msg_ref[z, 384:400, :] = tail


def left_body(recv_ref, left_ref, bsq_ref, msg_ref, asq_ref, new_ref=None):
    asq = unpack_rows(recv_ref[:, 384:400, :])
    alpha = jnp.sqrt(asq + EPS)
    beta = jnp.sqrt(bsq_ref[...] + EPS)
    total = recv_ref[0, 0:384, :].astype(F32)
    for z in range(1, 4):
        total = total + recv_ref[z, 0:384, :].astype(F32)
    fresh = total * (1.0 / alpha) - (alpha / beta) * left_ref[...].astype(F32)
    if new_ref is not None:
        new_ref[...] = fresh
    narrow = fresh.astype(BF)
    for z in range(4):
        msg_ref[z] = narrow
    asq_ref[...] = asq


def spread(slot_ref, rows_ref, tiles_ref, acc, half):
    for seg, top, rows, at in parts_of(half):
        chunk = rows_ref[pl.ds(at, rows), :]
        for j in range(2):
            acc[slot_ref[j, seg]] += lax.dot_general(
                chunk,
                tiles_ref[seg, j, pl.ds(top, rows), :],
                (((0,), (0,)), ((), ())),
                preferred_element_type=F32,
            )


def row_squares(ref):
    total = jnp.zeros((8, LANES), F32)
    for i in range(ref.shape[0] // 512):
        wide = ref[i * 512 : (i + 1) * 512, :].astype(F32)
        total = total + jnp.sum((wide * wide).reshape(64, 8, LANES), axis=0)
    return jnp.sum(total, axis=0, keepdims=True)


def write_pieces(msg_ref, tail, piece):
    for q in range(32):
        lane = (q % 4) * LANES
        msg_ref[q] = jnp.concatenate([piece(q // 4, lane), tail], axis=0).astype(BF)


def back_first_body(
    start_ref, slot_ref, rows_ref, tiles_in, msg_ref, tiles_ref, left_ref, acc, sem
):
    copy = pltpu.make_async_copy(tiles_in, tiles_ref, sem)
    copy.start()
    acc[...] = jnp.zeros_like(acc)
    left_ref[...] = rows_ref[pl.ds(pl.multiple_of(start_ref[0], 128), 384), :].astype(F32)
    tail = pack_row(row_squares(rows_ref), TAIL)
    for seg in range(3):
        for j in range(2):
            acc[slot_ref[j, seg]] += lax.dot_general(
                rows_ref[seg * 1024 : (seg + 1) * 1024, :],
                tiles_in[seg, j],
                (((0,), (0,)), ((), ())),
                preferred_element_type=F32,
            )
    write_pieces(msg_ref, tail, lambda p, lane: acc[p, :, lane : lane + LANES])
    copy.wait()


def back_own_body(core_ref, slot_ref, rows_ref, tiles_ref, acc_ref, bsq_ref):
    acc_ref[...] = jnp.zeros_like(acc_ref)
    spread(slot_ref, rows_ref, tiles_ref, acc_ref, core_ref[0])
    bsq_ref[...] = row_squares(rows_ref)


def back_other_body(core_ref, slot_ref, rows_ref, acc_ref, bsq_ref, tiles_ref, msg_ref, acc):
    spread(slot_ref, rows_ref, tiles_ref, acc, 1 - core_ref[0])
    tail = pack_row(row_squares(rows_ref) + bsq_ref[...], TAIL)
    write_pieces(msg_ref, tail, lambda p, lane: acc[p, :, lane : lane + LANES])


def share_body(first, last, recv_ref, *refs):
    if not first:
        prev_ref, asq_ref = refs[:2]
        refs = refs[2:]
    msg_ref, bsq_ref = refs[:2]
    total = recv_ref[0].astype(F32)
    for q in range(1, 32):
        total = total + recv_ref[q].astype(F32)
    bsq = jnp.sum(total[LANES : LANES + TAIL, :], axis=0, keepdims=True)
    beta = jnp.sqrt(bsq + EPS)
    fresh = total[0:LANES, :] * across(1.0 / beta)
    if not first:
        alpha = jnp.sqrt(asq_ref[...] + EPS)
        fresh = fresh - across(beta / alpha) * prev_ref[...]
    if not last:
        refs[2][...] = fresh
    narrow = jnp.transpose(fresh).astype(BF)
    for q in range(32):
        msg_ref[q] = narrow
    bsq_ref[...] = bsq


def square_body(g_ref, msg_ref):
    tile = pack_row(column_squares(g_ref)).astype(BF)
    for i in range(8):
        msg_ref[i] = tile


def coefficients(b0, b1, b2, b3, a0, a1, a2):
    beta = [jnp.sqrt(b[...] + EPS) for b in (b0, b1, b2, b3)]
    alpha = [jnp.sqrt(a[...] + EPS) for a in (a0, a1, a2)]
    phi_bar, rho_bar = beta[0], alpha[0]
    steps, shifts = [], []
    for k in range(ITERS):
        rho = jnp.sqrt(rho_bar * rho_bar + beta[k + 1] * beta[k + 1])
        cosine, sine = rho_bar / rho, beta[k + 1] / rho
        steps.append(cosine * phi_bar / rho)
        phi_bar = sine * phi_bar
        if k < ITERS - 1:
            shifts.append(sine * alpha[k + 1] / rho)
            rho_bar = -cosine * alpha[k + 1]
    s1, s2, s3 = steps
    t1, t2 = shifts
    rows = [
        (s1 - s2 * t1 + s3 * t2 * t1) / alpha[0],
        (s2 - s3 * t2) / alpha[1],
        s3 / alpha[2],
        t2 * t1 / alpha[0],
        -t2 / alpha[1],
        1.0 / alpha[2],
        sine / rho,
        jnp.zeros_like(s1),
    ]
    return jnp.concatenate(rows, axis=0), phi_bar


def final_body(*refs):
    asq_ref = refs[7]
    gathered = refs[8:12]
    sol_hbm, search_hbm, phi_ref, stage, sems = refs[12:]
    rows, phi_bar = coefficients(*refs[:7])
    phi_ref[...] = phi_bar
    alpha = jnp.sqrt(unpack_rows(asq_ref[...]) + EPS)
    older = -alpha * rows[6:7] * rows[3:6]
    newest = 1.0 / alpha
    copies = []
    for p in range(8):
        at = pl.ds(p * 512, 512)
        g0, g1, g2, g3 = [ref[p].astype(F32) for ref in gathered]
        stage[0, at, :] = rows[0:1] * g0 + rows[1:2] * g1 + rows[2:3] * g2
        stage[1, at, :] = older[0:1] * g0 + older[1:2] * g1 + older[2:3] * g2 + newest * g3
        for i, out in enumerate((sol_hbm, search_hbm)):
            copies.append(pltpu.make_async_copy(stage.at[i, at], out.at[at], sems.at[i, p]))
            copies[-1].start()
    for c in copies:
        c.wait()


def per_device(readings, design_tiles, pattern):
    tiles = design_tiles.reshape(3, 2, 1024, 512)
    slots = jnp.transpose(pattern, (1, 2, 0)).reshape(2, 3)
    basis = lax.axis_index("basis")
    core = lax.rem(basis, 2).reshape(1).astype(jnp.int32)
    z_hi = lax.div(basis, 2)
    acc_type = sds((8, LANES, 512), F32)
    row_type = sds((1, LANES), F32)
    msg_type = sds((32, LANES + TAIL, LANES), BF)
    acc_buf = pltpu.VMEM((8, LANES, 512), F32)

    send_half = call(send_body, [SM, SM, VM, VM], [sds((1552, LANES), BF), row_type], flops=4e8)
    keep_half = call(keep_body, [SM, SM, VM, VM], [sds((1536, LANES), F32)], flops=4e8)
    merge = call(merge_body, [VM] * 3, [sds((4, 400, LANES), BF)])
    left_outs = [sds((4, 384, LANES), BF), row_type, sds((384, LANES), F32)]
    left = call(left_body, [VM] * 3, left_outs)
    left_last = call(left_body, [VM] * 3, left_outs[:2])
    back_first = call(
        back_first_body,
        [SM, SM, VM, VM],
        [msg_type, sds((3, 2, 1024, 512), BF), sds((384, LANES), F32)],
        [acc_buf, pltpu.SemaphoreType.DMA(())],
        flops=8e8,
    )
    back_own = call(back_own_body, [SM, SM, VM, VM], [acc_type, row_type], flops=4e8)
    back_other = call(
        back_other_body, [SM, SM, VM, VM, VM, VM], [msg_type, acc_type], flops=4e8, aliases={3: 1}
    )
    share_outs = [sds((32, LANES, LANES), BF), row_type, sds((LANES, LANES), F32)]
    share_first = call(functools.partial(share_body, True, False), [VM], share_outs)
    share = call(functools.partial(share_body, False, False), [VM] * 3, share_outs)
    share_last = call(functools.partial(share_body, False, True), [VM] * 3, share_outs[:2])

    finish = pl.pallas_call(
        final_body,
        in_specs=[VM] * 12,
        out_specs=[ANY, ANY, VM],
        out_shape=[sds((4096, LANES), F32), sds((4096, LANES), F32), row_type],
        scratch_shapes=[pltpu.VMEM((2, 4096, LANES), F32), pltpu.SemaphoreType.DMA((2, 8))],
        compiler_params=pltpu.CompilerParams(vmem_limit_bytes=VMEM_LIMIT),
    )

    def gather(msg):
        return over_sensor(msg).reshape(8, 512, LANES)

    def over_sensor(msg):
        return lax.all_to_all(msg, "sensor", 0, 0, tiled=True, axis_index_groups=S_GROUPS)

    def over_z(msg):
        return lax.all_to_all(msg, "basis", 0, 0, tiled=True, axis_index_groups=Z_GROUPS)

    start = core * 1536 + (3 - z_hi.astype(jnp.int32)) * 384
    slots, core, start = lax.optimization_barrier((slots, core, start))
    msg, tiles, left_rows = back_first(start, slots, readings, tiles)
    msg, bsq, r = share_first(over_sensor(msg))
    gathered = [gather(msg)]
    bsqs = [bsq]
    asqs = []
    for sweep in range(ITERS):
        last = sweep == ITERS - 1
        send, asq = send_half(core, slots, gathered[-1], tiles)
        other = lax.ppermute(send, "basis", CORE_PERM)
        (keep,) = keep_half(core, slots, gathered[-1], tiles)
        (msg,) = merge(keep, other, asq)
        if last:
            msg, asq = left_last(over_z(msg), left_rows, bsqs[-1])
        else:
            msg, asq, left_rows = left(over_z(msg), left_rows, bsqs[-1])
        asqs.append(asq)
        own = over_z(msg).reshape(1536, LANES)
        other = lax.ppermute(own, "basis", CORE_PERM)
        acc, own_bsq = back_own(core, slots, own, tiles)
        msg, _ = back_other(core, slots, other, acc, own_bsq, tiles)
        if last:
            msg, bsq = share_last(over_sensor(msg), r, asq)
        else:
            msg, bsq, r = share(over_sensor(msg), r, asq)
        bsqs.append(bsq)
        gathered.append(gather(msg))
    (msg,) = call(square_body, [VM], [sds((8, EXTRA, LANES), BF)])(gathered[-1])
    msg = lax.all_to_all(msg, "basis", 0, 0, tiled=True)
    sol, search, phi_bar = finish(*bsqs, *asqs, msg, *gathered)
    return sol, search, phi_bar.reshape(LANES)


def solution(mesh):
    placed = (P("sensor", None), P("sensor", "basis", None, None, None), P("sensor", "basis", None))
    return jax.shard_map(
        per_device,
        mesh=mesh,
        in_specs=placed,
        out_specs=(P("basis", None), P("basis", None), P()),
        check_vma=False,
    )
```
